128 devices in a mesh: exp: 8 (over z, core), fsdp: 16 (over x, y).
Axes of the slice: x: 4, y: 4, z: 4, core: 2. Of those that a mesh axis runs over, the one named last changes fastest.
Arguments:
- tokens: bfloat16 [2048, 3072], P('fsdp'), may hold values from -6 to 6
- router_weight: bfloat16 [3072, 8], replicated, may hold values from -0.109375 to 0.109375
- expert_ids: int32 [2048, 2], P('fsdp'), may hold values from 0 to 7, all different within a row; in each aligned block of 128 rows (0 to 127, 128 to 255, ...) at most 40 rows name the same one
- expert_gate: bfloat16 [8, 3072, 8192], P('exp', None, 'fsdp'), may hold values from -0.109375 to 0.109375
- expert_up: bfloat16 [8, 3072, 8192], P('exp', None, 'fsdp'), may hold values from -0.109375 to 0.109375
- expert_down: bfloat16 [8, 8192, 3072], P('exp', 'fsdp'), may hold values from -0.0625 to 0.0625
- gate_weight: bfloat16 [3072, 8192], P('fsdp', 'exp'), may hold values from -0.109375 to 0.109375
- up_weight: bfloat16 [3072, 8192], P('fsdp', 'exp'), may hold values from -0.109375 to 0.109375
- down_weight: bfloat16 [8192, 3072], P('exp', 'fsdp'), may hold values from -0.0625 to 0.0625
Outputs:
- grad_gate: float32 [3072, 8192], P('fsdp', 'exp')
- grad_up: float32 [3072, 8192], P('fsdp', 'exp')
- grad_down: float32 [8192, 3072], P('exp', 'fsdp')
The draws below stay inside these ranges and needn't reach their ends.
Inputs may be any that keep to these rules, and one draw needn't show every extreme that they name: `expert_ids`: each row names 2 different experts. In the 128 rows of one fsdp block no expert is named by more than 40 rows, and in every draw some expert of some block is named by exactly 40.
All inputs are finite; a program needn't handle non-finite values.
Results may differ from the reference program's by a relative error of at most 0.022.
Values may be sent and summed in bfloat16 or wider, within the bound.
No kernel may reach another device: no remote copies, remote signals or barrier semaphores. Data moves between devices by JAX's collectives and lax.ppermute only.
A program may use at most 192 MiB of HBM per device.

```python
import math
import jax
import jax.numpy as jnp
import numpy as np
from jax import lax

D = 3072
FF_E = 8192
FF_S = 8192
TOP = 2
TOK_DEV = 128
EXPERTS = 8
CAP = 40
TOKENS = 2048
N_FSDP = 16


def shard_levels(stream_key, shape, shards, low, high):
    level = 1.0
    for dim, blocks in shards:
        heights = jax.random.uniform(jax.random.fold_in(jax.random.fold_in(stream_key, 6), dim), (blocks,), jnp.float32, low / len(shards), high / len(shards))
        level = level * jnp.repeat(jnp.exp(heights), shape[dim] // blocks).reshape((-1,) + (1,) * (len(shape) - 1 - dim))
    return level


def assign_block(stream_key, own, number, rows, number_of, top, most, slope):
    order = jax.random.permutation(stream_key, number_of)
    heavy_load, ordinary = shares(number_of, rows * top, most, slope, True), shares(number_of, rows * top, most, slope, False)
    places = jnp.arange(number_of)

    def named(lengths, turn):
        used = int((lengths > 0).sum())
        fixed = max(1, used // 4)
        passed = fixed + (places - fixed + turn * (used - fixed)) % max(1, number_of - fixed)
        return jnp.zeros((number_of,), jnp.int32).at[order[jnp.where(places < fixed, places, passed)]].set(jnp.asarray(lengths, jnp.int32))

    lengths = jnp.where(number % 4 == 0, named(heavy_load, number // 4), named(ordinary, number - number // 4 - 1))
    mixed = jax.random.permutation(jax.random.fold_in(own, 3), number_of)
    source_of, receiver = mixed[0:number_of // 2 * 2:2], mixed[1:number_of // 2 * 2:2]
    margin = jnp.minimum(lengths[source_of] - 1, most - lengths[receiver]) // 2
    margin = jnp.where((source_of == order[0]) | (receiver == order[0]) | (lengths[receiver] == 0), 0, jnp.maximum(margin, 0))
    passed = jax.random.randint(jax.random.fold_in(own, 4), (number_of // 2,), 0, 1 << 20) % (margin + 1)
    lengths = lengths.at[source_of].add(-passed).at[receiver].add(passed)
    items = jnp.searchsorted(jnp.cumsum(lengths), jnp.arange(rows * top), side="right").astype(jnp.int32)
    table = items.reshape(top, rows).T
    table = table[jax.random.permutation(jax.random.fold_in(own, 1), rows)]
    turn = jax.random.randint(jax.random.fold_in(own, 2), (rows, 1), 0, top)
    return jnp.take_along_axis(table, (jnp.arange(top)[None, :] + turn) % top, axis=1)


def shares(amount, total, limit, slope, full):
    portions = [(1 << 20) // math.isqrt(grade ** slope) + 1 for grade in range(1, amount + 1)]
    largest = limit if full else min(limit, max(-(-total // amount), total * portions[0] // sum(portions)))
    least = 1 if total - largest >= amount - 1 else 0
    counts, surplus = [largest] + [least] * (amount - 1), total - largest - least * (amount - 1)
    while surplus > 0:
        free = [i for i in range(1, amount) if counts[i] < largest] or [i for i in range(1, amount) if counts[i] < limit]
        whole, left = sum([portions[i] for i in free]), surplus
        for i in free:
            extra = min(limit - counts[i], max(1, left * portions[i] // whole), surplus)
            counts[i] = counts[i] + extra
            surplus = surplus - extra
    return np.array(counts)


def noise(rng, shape, scale, reach, pieces=(), kind=jnp.bfloat16):
    entries = jax.random.normal(rng, shape, jnp.float32) * scale
    if len(pieces) > 0:
        entries = shard_levels(rng, shape, pieces, -0.22, 0.18) * entries
    return jnp.clip(entries, min=-reach, max=reach).astype(kind)


def setup_inputs(seed: int = 0) -> dict:
    key_list = jax.random.split(jax.random.key(seed), 10)
    tokens = noise(key_list[0], (TOKENS, D), 1.0, 6.0, ((0, 16),))
    router_weight = noise(key_list[1], (D, EXPERTS), D ** -0.5, 0.109375)
    expert_ids_keys = jax.random.split(jax.random.fold_in(key_list[2], 1), TOKENS // TOK_DEV)
    expert_ids_turns = jax.random.permutation(jax.random.fold_in(key_list[2], 3), TOKENS // TOK_DEV)
    expert_ids = jax.vmap(lambda own, number: assign_block(jax.random.fold_in(key_list[2], 2), own, number, TOK_DEV, EXPERTS, TOP, CAP, 2))(expert_ids_keys, expert_ids_turns).reshape((TOKENS, TOP))
    expert_gate = noise(key_list[3], (EXPERTS, D, FF_E), D ** -0.5, 0.109375, ((0, 8), (2, 16)))
    expert_up = noise(key_list[4], (EXPERTS, D, FF_E), D ** -0.5, 0.109375, ((0, 8), (2, 16)))
    expert_down = noise(key_list[5], (EXPERTS, FF_E, D), FF_E ** -0.5, 0.0625, ((0, 8), (1, 16)))
    gate_weight = noise(key_list[6], (D, FF_S), D ** -0.5, 0.109375, ((0, 16), (1, 8)))
    up_weight = noise(key_list[7], (D, FF_S), D ** -0.5, 0.109375, ((0, 16), (1, 8)))
    down_weight = noise(key_list[8], (FF_S, D), FF_S ** -0.5, 0.0625, ((0, 8), (1, 16)))
    return {"tokens": tokens, "router_weight": router_weight, "expert_ids": expert_ids, "expert_gate": expert_gate, "expert_up": expert_up, "expert_down": expert_down, "gate_weight": gate_weight, "up_weight": up_weight, "down_weight": down_weight}


def gate_mix(tokens, router_weight, expert_ids):
    logits = jnp.dot(tokens, router_weight, preferred_element_type=jnp.float32)
    experts_count = router_weight.shape[1]
    onehot = (expert_ids[:, :, None] == jnp.arange(experts_count, dtype=jnp.int32)[None, None, :]).astype(jnp.float32)
    picked_logits = lax.optimization_barrier(jnp.sum(onehot * logits[:, None, :], axis=2))
    return 1.0 / (1.0 + jnp.exp(picked_logits[:, ::-1] - picked_logits))

def slot_table(expert_ids):
    flat_ids = expert_ids.reshape(N_FSDP, TOK_DEV * TOP)
    onehot = (flat_ids[:, :, None] == jnp.arange(EXPERTS, dtype=jnp.int32)[None, None, :]).astype(jnp.int32)
    before = jnp.cumsum(onehot, axis=1) - onehot
    return lax.optimization_barrier(jnp.sum(before * onehot, axis=2)).reshape(TOKENS, TOP).astype(jnp.int32)

def reference(tokens, router_weight, expert_ids, expert_gate, expert_up, expert_down, gate_weight, up_weight, down_weight):
    mixing = gate_mix(tokens, router_weight, expert_ids)
    slot_index = slot_table(expert_ids)
    block_ids = (jnp.arange(TOKENS, dtype=jnp.int32) // TOK_DEV).astype(jnp.int32)
    dest_row = block_ids[:, None] * CAP + slot_index
    buffer_rows = N_FSDP * CAP
    token_pairs = jnp.broadcast_to(tokens[:, None, :], (TOKENS, TOP, D)).reshape(TOKENS * TOP, D)

    def one_expert(summed, inputs):
        w_gate, w_up, w_down, number = inputs
        chosen = expert_ids == number
        target = jnp.where(chosen, dest_row, buffer_rows).astype(jnp.int32)
        buffer = jnp.zeros((buffer_rows, D), jnp.bfloat16)
        buffer = buffer.at[target.reshape(-1)].set(token_pairs, mode='drop')
        pre_gate = jnp.dot(buffer, w_gate, preferred_element_type=jnp.float32)
        pre_up = jnp.dot(buffer, w_up, preferred_element_type=jnp.float32)
        hidden = (jax.nn.silu(pre_gate) * pre_up).astype(jnp.bfloat16)
        groups = hidden.reshape(buffer_rows, N_FSDP, FF_E // N_FSDP).astype(jnp.float32)
        w_split = w_down.reshape(N_FSDP, FF_E // N_FSDP, D).astype(jnp.float32)
        partial_value = jnp.einsum('rsh,shd->srd', groups, w_split)
        rounded = lax.optimization_barrier(partial_value.astype(jnp.bfloat16))
        expert_out = lax.optimization_barrier(jnp.sum(rounded.astype(jnp.float32), axis=0))
        picked = jnp.take(expert_out, jnp.minimum(target, buffer_rows - 1), axis=0)
        weight = jnp.where(chosen, mixing, jnp.zeros_like(mixing))
        summed = summed + lax.optimization_barrier(jnp.sum(weight[:, :, None] * picked, axis=1))
        return (summed, None)
    numbers = jnp.arange(EXPERTS, dtype=jnp.int32)
    teacher, unused = lax.scan(one_expert, jnp.zeros((TOKENS, D), jnp.float32), (expert_gate, expert_up, expert_down, numbers))
    pre_act = jnp.dot(tokens, gate_weight, preferred_element_type=jnp.float32)
    up_proj = jnp.dot(tokens, up_weight, preferred_element_type=jnp.float32)
    active = jax.nn.silu(pre_act)
    hidden = (active * up_proj).astype(jnp.bfloat16)
    student = jnp.dot(hidden, down_weight, preferred_element_type=jnp.float32)
    loss_scale = 1.0 / jnp.sqrt(jnp.float32(TOKENS))
    grad_out = ((student - teacher) * loss_scale).astype(jnp.bfloat16)
    grad_hidden = lax.dot_general(grad_out, down_weight, (((1,), (1,)), ((), ())), preferred_element_type=jnp.float32)
    sig_gate = jax.nn.sigmoid(pre_act)
    grad_pre = (grad_hidden * up_proj * sig_gate * (1.0 + pre_act * (1.0 - sig_gate))).astype(jnp.bfloat16)
    grad_upper = (grad_hidden * active).astype(jnp.bfloat16)
    contract = (((0,), (0,)), ((), ()))
    grad_gate = lax.dot_general(tokens, grad_pre, contract, preferred_element_type=jnp.float32)
    grad_up = lax.dot_general(tokens, grad_upper, contract, preferred_element_type=jnp.float32)
    grad_down = lax.dot_general(hidden, grad_out, contract, preferred_element_type=jnp.float32)
    return (grad_gate, grad_up, grad_down)
```

```python
import jax
import jax.numpy as jnp
from jax import lax
from jax.sharding import Mesh, PartitionSpec as P

F32 = jnp.float32
BF16 = jnp.bfloat16


def gate_mix(tokens, router_weight, expert_ids):
    logits = jnp.dot(tokens, router_weight, preferred_element_type=F32)
    experts_count = router_weight.shape[1]
    onehot = (
        expert_ids[:, :, None] == jnp.arange(experts_count, dtype=jnp.int32)[None, None, :]
    ).astype(F32)
    picked_logits = jnp.sum(onehot * logits[:, None, :], axis=2)
    return 1.0 / (1.0 + jnp.exp(picked_logits[:, ::-1] - picked_logits))


def local_slots(expert_ids, experts_count):
    pairs = expert_ids.shape[0] * expert_ids.shape[1]
    flat_ids = expert_ids.reshape(pairs)
    onehot = (flat_ids[:, None] == jnp.arange(experts_count, dtype=jnp.int32)[None, :]).astype(
        jnp.int32
    )
    before = jnp.cumsum(onehot, axis=0) - onehot
    return jnp.sum(before * onehot, axis=1).reshape(expert_ids.shape)


def shift(value, axis, step):
    size = lax.axis_size(axis)
    return lax.ppermute(value, axis, [(i, (i + step) % size) for i in range(size)])


def gather_direct(value, axis):
    return [value, shift(value, axis, -1), shift(value, axis, -2), shift(value, axis, -3)]


def gather_ring(value, axis):
    behind = shift(value, axis, 1)
    ahead = shift(value, axis, -1)
    half = value.shape[0] // 2
    far = jnp.concatenate(
        [shift(behind[:half], axis, 1), shift(ahead[half:], axis, -1)], axis=0
    )
    return [value, ahead, far, behind]


def send_direct(pieces, axis):
    return [
        pieces[0],
        shift(pieces[3], axis, -1),
        shift(pieces[2], axis, -2),
        shift(pieces[1], axis, 1),
    ]


def scatter_direct(pieces, axis):
    own = pieces[0].astype(F32)
    sent = send_direct([None] + [p.astype(BF16) for p in pieces[1:]], axis)
    return own + sent[1].astype(F32) + sent[2].astype(F32) + sent[3].astype(F32)


def scatter_ring(pieces, axis):
    half = pieces[2].shape[0] // 2
    far = pieces[2].astype(BF16)
    up = shift(far[:half], axis, 1)
    down = shift(far[half:], axis, -1)
    ahead = pieces[1].astype(F32)
    ahead = jnp.concatenate([ahead[:half] + up.astype(F32), ahead[half:]], axis=0).astype(BF16)
    behind = pieces[3].astype(F32)
    behind = jnp.concatenate(
        [behind[:half], behind[half:] + down.astype(F32)], axis=0
    ).astype(BF16)
    from_behind = shift(ahead, axis, 1)
    from_ahead = shift(behind, axis, -1)
    return pieces[0].astype(F32) + from_behind.astype(F32) + from_ahead.astype(F32)


def body(
    tokens,
    router_weight,
    expert_ids,
    expert_gate,
    expert_up,
    expert_down,
    gate_weight,
    up_weight,
    down_weight,
):
    rows, width = tokens.shape
    experts_count = router_weight.shape[1]
    capacity = rows * expert_ids.shape[1] * 5 // (4 * experts_count)
    part, units = gate_weight.shape
    block = units // 4
    half = width // 2
    ix, iy, iz, ic = (lax.axis_index(a) for a in ("x", "y", "z", "core"))
    number = iz * 2 + ic

    def swap(value):
        return shift(value, "core", 1)

    mixing = gate_mix(tokens, router_weight, expert_ids)
    slot_index = local_slots(expert_ids, experts_count)
    chosen = expert_ids == number
    slot_range = jnp.arange(capacity, dtype=jnp.int32)
    matches = chosen[None, :, :] & (slot_index[None, :, :] == slot_range[:, None, None])
    placing = jnp.any(matches, axis=2).astype(BF16)
    weighting = jnp.sum(jnp.where(matches, mixing[None, :, :], 0.0), axis=2)
    buffer = jnp.dot(placing, tokens, preferred_element_type=F32).astype(BF16)
    column = jnp.stack(gather_direct(buffer, "y")).reshape(4 * capacity, width)
    arrived = gather_ring(column, "x")
    w_gate, w_up, w_down = expert_gate[0], expert_up[0], expert_down[0]
    hidden_rows = []
    for rows_x in arrived:
        pre_gate = jnp.dot(rows_x, w_gate, preferred_element_type=F32)
        pre_up = jnp.dot(rows_x, w_up, preferred_element_type=F32)
        hidden_rows.append((jax.nn.silu(pre_gate) * pre_up).astype(BF16))
    hidden_rows = jnp.stack(hidden_rows).reshape(4, 4, capacity, -1)
    outs = [
        jnp.dot(
            hidden_rows[:, k].reshape(4 * capacity, -1), w_down, preferred_element_type=F32
        ).astype(BF16)
        for k in range(4)
    ]
    out_y = scatter_ring(outs, "y").reshape(4, capacity, width)
    expert_out = scatter_direct([out_y[k] for k in range(4)], "x")

    packed = jnp.concatenate(
        [
            gate_weight.reshape(part, 4, 1, block),
            up_weight.reshape(part, 4, 1, block),
            down_weight.T.reshape(part, 4, 1, block),
        ],
        axis=2,
    ).reshape(part, 4, 3 * block)
    pieces = [
        lax.dynamic_index_in_dim(packed, (ix + k) % 4, axis=1, keepdims=False) for k in range(4)
    ]
    across = send_direct(pieces, "x")
    weights_x = jnp.zeros((4, part, 3 * block), BF16)
    for k in range(4):
        place = ((ix + k) % 4) ^ (2 * ic)
        weights_x = lax.dynamic_update_index_in_dim(weights_x, across[k], place, 0)
    weights = jnp.zeros((4, 4, part, 3 * block), BF16)
    for k, piece in enumerate(gather_ring(weights_x, "y")):
        weights = lax.dynamic_update_index_in_dim(weights, piece, (iy + k) % 4, 1)
    weights = weights.reshape(width, 3 * block)
    w_in = weights[:, : 2 * block]
    w_out = weights[:, 2 * block :]

    turned = jnp.roll(tokens, -iz * (rows // 4), axis=0)
    mine = lax.dynamic_slice_in_dim(turned, ic * half, half, axis=1)
    tokens_own = jnp.concatenate(gather_ring(mine, "x"), axis=0)
    tokens_all = jnp.concatenate([tokens_own, swap(tokens_own)], axis=1)
    pre = jnp.dot(tokens_all, w_in, preferred_element_type=F32)
    pre_act, up_proj = pre[:, :block], pre[:, block:]
    sig_gate = jax.nn.sigmoid(pre_act)
    active = pre_act * sig_gate
    hidden = (active * up_proj).astype(BF16)
    nt = (((1,), (1,)), ((), ()))
    tn = (((0,), (0,)), ((), ()))
    student_other = lax.dot_general(
        hidden, w_out[half:], nt, preferred_element_type=F32
    ).astype(BF16)
    student_own = lax.dot_general(hidden, w_out[:half], nt, preferred_element_type=F32)
    student = (student_own + swap(student_other).astype(F32)).reshape(4, rows, half)
    student = scatter_direct([student[k] for k in range(4)], "x")

    weighting = jnp.roll(weighting, -iz * (rows // 4), axis=1)
    halves = [
        lax.dynamic_slice_in_dim(expert_out, (ic if own else 1 - ic) * half, half, axis=1)
        for own in (True, False)
    ]
    teacher_own, teacher_other = [
        lax.dot_general(
            weighting, h, tn, precision=lax.Precision.HIGHEST, preferred_element_type=F32
        )
        for h in halves
    ]
    teacher = teacher_own + swap(teacher_other.astype(BF16)).astype(F32)
    partial_value = (student - teacher).reshape(4, rows // 4, half)
    total = scatter_direct([partial_value[k] for k in range(4)], "z")
    token_total = rows * 16
    loss_scale = 1.0 / jnp.sqrt(jnp.float32(token_total))
    grad_out = (total * loss_scale).astype(BF16)
    grad_out = jnp.concatenate(gather_direct(grad_out, "z"), axis=0)
    grad_own = jnp.concatenate(gather_ring(grad_out, "x"), axis=0)
    grad_all = jnp.concatenate([grad_own, swap(grad_own)], axis=1)

    grad_down = lax.dot_general(grad_all, hidden, tn, preferred_element_type=F32)
    grad_hidden = jnp.dot(grad_all, w_out, preferred_element_type=F32)
    grad_pre = (grad_hidden * up_proj * sig_gate * (1.0 + pre_act * (1.0 - sig_gate))).astype(
        BF16
    )
    grad_upper = (grad_hidden * active).astype(BF16)
    grad_gate = lax.dot_general(tokens_all, grad_pre, tn, preferred_element_type=F32)
    grad_up = lax.dot_general(tokens_all, grad_upper, tn, preferred_element_type=F32)

    def finish(grad):
        grad = grad.astype(BF16).reshape(4, 4, part, block)
        pieces = [
            lax.dynamic_index_in_dim(grad, (iy + k) % 4, axis=1, keepdims=False)
            for k in range(4)
        ]
        summed = scatter_ring(pieces, "y")
        pieces = [
            lax.dynamic_index_in_dim(
                summed, ((ix + k) % 4) ^ (2 * ic), axis=0, keepdims=False
            ).astype(F32 if k == 0 else BF16)
            for k in range(4)
        ]
        parts = [p.astype(F32) for p in send_direct(pieces, "x")]
        return jnp.concatenate(
            [lax.select_n((place - ix) % 4, *parts) for place in range(4)], axis=1
        )

    return (finish(grad_gate), finish(grad_up), finish(grad_down).T)


def solution(mesh):
    parts = Mesh(mesh.devices.reshape(4, 2, 4, 4), ("z", "core", "x", "y"))
    exp, fsdp = ("z", "core"), ("x", "y")
    return jax.shard_map(
        body,
        mesh=parts,
        in_specs=(
            P(fsdp, None),
            P(),
            P(fsdp, None),
            P(exp, None, fsdp),
            P(exp, None, fsdp),
            P(exp, fsdp, None),
            P(fsdp, exp),
            P(fsdp, exp),
            P(exp, fsdp),
        ),
        out_specs=(P(fsdp, exp), P(fsdp, exp), P(exp, fsdp)),
        check_vma=False,
    )
```

```python
import jax
import jax.numpy as jnp
from jax import lax
from jax.sharding import Mesh, PartitionSpec as P

F32 = jnp.float32
BF16 = jnp.bfloat16


def gate_mix(tokens, router_weight, expert_ids):
    logits = jnp.dot(tokens, router_weight, preferred_element_type=F32)
    experts_count = router_weight.shape[1]
    onehot = (
        expert_ids[:, :, None] == jnp.arange(experts_count, dtype=jnp.int32)[None, None, :]
    ).astype(F32)
    picked_logits = jnp.sum(onehot * logits[:, None, :], axis=2)
    return 1.0 / (1.0 + jnp.exp(picked_logits[:, ::-1] - picked_logits))


def local_slots(expert_ids, experts_count):
    pairs = expert_ids.shape[0] * expert_ids.shape[1]
    flat_ids = expert_ids.reshape(pairs)
    onehot = (flat_ids[:, None] == jnp.arange(experts_count, dtype=jnp.int32)[None, :]).astype(
        jnp.int32
    )
    before = jnp.cumsum(onehot, axis=0) - onehot
    return jnp.sum(before * onehot, axis=1).reshape(expert_ids.shape)


def shift(value, axis, step):
    size = lax.axis_size(axis)
    return lax.ppermute(value, axis, [(i, (i + step) % size) for i in range(size)])


def gather_direct(value, axis):
    return [value, shift(value, axis, -1), shift(value, axis, -2), shift(value, axis, -3)]


def gather_ring(value, axis):
    behind = shift(value, axis, 1)
    ahead = shift(value, axis, -1)
    half = value.shape[0] // 2
    far = jnp.concatenate(
        [shift(behind[:half], axis, 1), shift(ahead[half:], axis, -1)], axis=0
    )
    return [value, ahead, far, behind]


def send_direct(pieces, axis):
    return [
        pieces[0],
        shift(pieces[3], axis, -1),
        shift(pieces[2], axis, -2),
        shift(pieces[1], axis, 1),
    ]


def scatter_direct(pieces, axis):
    own = pieces[0].astype(F32)
    sent = send_direct([None] + [p.astype(BF16) for p in pieces[1:]], axis)
    return own + sent[1].astype(F32) + sent[2].astype(F32) + sent[3].astype(F32)


def scatter_ring(pieces, axis):
    half = pieces[2].shape[0] // 2
    far = pieces[2].astype(BF16)
    up = shift(far[:half], axis, 1)
    down = shift(far[half:], axis, -1)
    ahead = pieces[1].astype(F32)
    ahead = jnp.concatenate([ahead[:half] + up.astype(F32), ahead[half:]], axis=0).astype(BF16)
    behind = pieces[3].astype(F32)
    behind = jnp.concatenate(
        [behind[:half], behind[half:] + down.astype(F32)], axis=0
    ).astype(BF16)
    from_behind = shift(ahead, axis, 1)
    from_ahead = shift(behind, axis, -1)
    return pieces[0].astype(F32) + from_behind.astype(F32) + from_ahead.astype(F32)


def body(
    tokens,
    router_weight,
    expert_ids,
    expert_gate,
    expert_up,
    expert_down,
    gate_weight,
    up_weight,
    down_weight,
):
    rows, width = tokens.shape
    experts_count = router_weight.shape[1]
    capacity = rows * expert_ids.shape[1] * 5 // (4 * experts_count)
    part, units = gate_weight.shape
    block = units // 4
    half = width // 2
    ix, iy, iz, ic = (lax.axis_index(a) for a in ("x", "y", "z", "core"))
    number = iz * 2 + ic

    def swap(value):
        return shift(value, "core", 1)

    chosen = expert_ids == number
    slot_index = local_slots(expert_ids, experts_count)
    slot_range = jnp.arange(capacity, dtype=jnp.int32)
    matches = chosen[None, :, :] & (slot_index[None, :, :] == slot_range[:, None, None])
    placing = jnp.any(matches, axis=2).astype(BF16)
    buffer = jnp.dot(placing, tokens, preferred_element_type=F32).astype(BF16)
    column = jnp.concatenate(gather_direct(buffer, "y"), axis=0)
    arrived = gather_ring(column, "x")
    tokens, buffer = lax.optimization_barrier((tokens, buffer))

    def packed(place):
        start = place * block
        return jnp.concatenate(
            [
                lax.dynamic_slice_in_dim(gate_weight, start, block, axis=1),
                lax.dynamic_slice_in_dim(up_weight, start, block, axis=1),
                lax.dynamic_slice_in_dim(down_weight, start, block, axis=0).T,
            ],
            axis=1,
        )

    across = send_direct([packed((ix + k) % 4) for k in range(4)], "x")
    weights_x = jnp.zeros((4, part, 3 * block), BF16)
    for k in range(4):
        place = ((ix + k) % 4) ^ (2 * ic)
        weights_x = lax.dynamic_update_index_in_dim(weights_x, across[k], place, 0)
    weights = jnp.zeros((4, 4, part, 3 * block), BF16)
    for k, piece in enumerate(gather_ring(weights_x, "y")):
        weights = lax.dynamic_update_index_in_dim(weights, piece, (iy + k) % 4, 1)
    weights = weights.reshape(width, 3 * block)
    w_in = weights[:, : 2 * block]
    w_out = weights[:, 2 * block :]

    mine = lax.dynamic_slice_in_dim(tokens, ic * half, half, axis=1)
    tokens_own = jnp.zeros((4, rows, half), BF16)
    for k, piece in enumerate(gather_direct(mine, "x")):
        tokens_own = lax.dynamic_update_index_in_dim(tokens_own, piece, (ix + k) % 4, 0)
    tokens_own = tokens_own.reshape(4 * rows, half)
    tokens_all = jnp.concatenate([tokens_own, swap(tokens_own)], axis=1)
    pre = jnp.dot(tokens_all, w_in, preferred_element_type=F32)
    pre_act, up_proj = pre[:, :block], pre[:, block:]
    sig_gate = jax.nn.sigmoid(pre_act)
    active = pre_act * sig_gate
    hidden = (active * up_proj).astype(BF16)
    nt = (((1,), (1,)), ((), ()))
    tn = (((0,), (0,)), ((), ()))
    student_other = lax.dot_general(
        hidden, w_out[half:], nt, preferred_element_type=F32
    ).astype(BF16)
    student_own = lax.dot_general(hidden, w_out[:half], nt, preferred_element_type=F32)
    student = (student_own + swap(student_other).astype(F32)).reshape(4, rows, half)
    student = scatter_direct(
        [
            lax.dynamic_index_in_dim(student, (ix + k) % 4, axis=0, keepdims=False)
            for k in range(4)
        ],
        "x",
    )

    w_gate, w_up, w_down = expert_gate[0], expert_up[0], expert_down[0]
    hidden_rows = []
    for rows_x in arrived:
        pre_gate = jnp.dot(rows_x, w_gate, preferred_element_type=F32)
        pre_up = jnp.dot(rows_x, w_up, preferred_element_type=F32)
        hidden_rows.append((jax.nn.silu(pre_gate) * pre_up).astype(BF16))
    along_x = [
        jnp.dot(h, w_down[:, half:], preferred_element_type=F32).astype(BF16)
        for h in hidden_rows
    ]
    along_y = [
        jnp.dot(
            jnp.concatenate(
                [h[k * capacity : (k + 1) * capacity] for h in hidden_rows], axis=0
            ),
            w_down[:, :half],
            preferred_element_type=F32,
        ).astype(BF16)
        for k in range(4)
    ]
    sum_x = scatter_direct(along_x, "x").reshape(4, capacity, half)
    sum_y = scatter_direct(along_y, "y").reshape(4, capacity, half)
    first = scatter_direct([sum_y[k] for k in range(4)], "x")
    second = scatter_direct([sum_x[k] for k in range(4)], "y")

    mixing = gate_mix(tokens, router_weight, expert_ids)
    weighting = jnp.sum(jnp.where(matches, mixing[None, :, :], 0.0), axis=2)
    teacher_first, teacher_second = [
        lax.dot_general(
            weighting, h, tn, precision=lax.Precision.HIGHEST, preferred_element_type=F32
        )
        for h in (first, second)
    ]
    teacher_own = jnp.where(ic == 0, teacher_first, teacher_second)
    teacher_other = jnp.where(ic == 0, teacher_second, teacher_first)
    teacher = teacher_own + swap(teacher_other.astype(BF16)).astype(F32)
    partial_value = (student - teacher).reshape(4, rows // 4, half)
    total = scatter_direct(
        [
            lax.dynamic_index_in_dim(partial_value, (iz + k) % 4, axis=0, keepdims=False)
            for k in range(4)
        ],
        "z",
    )
    token_total = rows * 16
    loss_scale = 1.0 / jnp.sqrt(jnp.float32(token_total))
    grad_out = (total * loss_scale).astype(BF16)
    grad_own = lax.all_to_all(
        jnp.broadcast_to(grad_out[None], (16,) + grad_out.shape), ("x", "z"), 0, 0
    ).reshape(4 * rows, half)
    grad_other = swap(grad_own)

    grad_hidden = jnp.dot(grad_own, w_out[:half], preferred_element_type=F32) + jnp.dot(
        grad_other, w_out[half:], preferred_element_type=F32
    )
    grad_down = jnp.concatenate(
        [
            lax.dot_general(g, hidden, tn, preferred_element_type=F32).astype(BF16)
            for g in (grad_own, grad_other)
        ],
        axis=0,
    )
    grad_pre = (grad_hidden * up_proj * sig_gate * (1.0 + pre_act * (1.0 - sig_gate))).astype(
        BF16
    )
    grad_upper = (grad_hidden * active).astype(BF16)
    grad_in = lax.dot_general(
        tokens_all,
        jnp.concatenate([grad_pre, grad_upper], axis=1),
        tn,
        preferred_element_type=F32,
    ).astype(BF16)

    def finish(grad):
        size = grad.shape[1]
        grad = grad.reshape(4, 4, part, size)
        pieces = [
            lax.dynamic_index_in_dim(grad, (iy + k) % 4, axis=1, keepdims=False)
            for k in range(4)
        ]
        summed = scatter_ring(pieces, "y")
        pieces = [
            lax.dynamic_index_in_dim(
                summed, ((ix + k) % 4) ^ (2 * ic), axis=0, keepdims=False
            ).astype(F32 if k == 0 else BF16)
            for k in range(4)
        ]
        parts = [p.astype(F32) for p in send_direct(pieces, "x")]
        placed = [lax.select_n((place - ix) % 4, *parts) for place in range(4)]
        return [
            jnp.concatenate([p[:, s : s + block] for p in placed], axis=1)
            for s in range(0, size, block)
        ]

    (down,) = finish(grad_down)
    gate, up = finish(grad_in)
    return (gate, up, down.T)


def solution(mesh):
    parts = Mesh(mesh.devices.reshape(4, 2, 4, 4), ("z", "core", "x", "y"))
    exp, fsdp = ("z", "core"), ("x", "y")
    return jax.shard_map(
        body,
        mesh=parts,
        in_specs=(
            P(fsdp, None),
            P(),
            P(fsdp, None),
            P(exp, None, fsdp),
            P(exp, None, fsdp),
            P(exp, fsdp, None),
            P(fsdp, exp),
            P(fsdp, exp),
            P(exp, fsdp),
        ),
        out_specs=(P(fsdp, exp), P(fsdp, exp), P(exp, fsdp)),
        check_vma=False,
    )
```

```python
import jax
import jax.numpy as jnp
from jax import lax
from jax.sharding import Mesh, PartitionSpec as P

F32 = jnp.float32
BF16 = jnp.bfloat16


def gate_mix(tokens, router_weight, expert_ids):
    logits = jnp.dot(tokens, router_weight, preferred_element_type=F32)
    experts_count = router_weight.shape[1]
    onehot = (
        expert_ids[:, :, None] == jnp.arange(experts_count, dtype=jnp.int32)[None, None, :]
    ).astype(F32)
    picked_logits = jnp.sum(onehot * logits[:, None, :], axis=2)
    return 1.0 / (1.0 + jnp.exp(picked_logits[:, ::-1] - picked_logits))


def local_slots(expert_ids, experts_count):
    pairs = expert_ids.shape[0] * expert_ids.shape[1]
    flat_ids = expert_ids.reshape(pairs)
    onehot = (flat_ids[:, None] == jnp.arange(experts_count, dtype=jnp.int32)[None, :]).astype(
        jnp.int32
    )
    before = jnp.cumsum(onehot, axis=0) - onehot
    return jnp.sum(before * onehot, axis=1).reshape(expert_ids.shape)


def shift(value, axis, step):
    size = lax.axis_size(axis)
    return lax.ppermute(value, axis, [(i, (i + step) % size) for i in range(size)])


def gather_direct(value, axis):
    return [value, shift(value, axis, -1), shift(value, axis, -2), shift(value, axis, -3)]


def after(value, *others):
    return lax.optimization_barrier((value, others))[0]


def gather_near(value, axis):
    return shift(value, axis, 1), shift(value, axis, -1)


def gather_far(near, axis):
    behind, ahead = near
    half = behind.shape[0] // 2
    return jnp.concatenate([shift(behind[:half], axis, 1), shift(ahead[half:], axis, -1)], axis=0)


def send_direct(pieces, axis):
    return [
        pieces[0],
        shift(pieces[3], axis, -1),
        shift(pieces[2], axis, -2),
        shift(pieces[1], axis, 1),
    ]


def scatter_direct(pieces, axis):
    own = pieces[0].astype(F32)
    sent = send_direct([None] + [p.astype(BF16) for p in pieces[1:]], axis)
    return own + sent[1].astype(F32) + sent[2].astype(F32) + sent[3].astype(F32)


def scatter_ring(pieces, axis, ahead_of=()):
    half = pieces[2].shape[0] // 2
    far = pieces[2].astype(BF16)
    up = shift(far[:half], axis, 1)
    down = shift(far[half:], axis, -1)
    ahead = pieces[1].astype(F32)
    ahead = jnp.concatenate([ahead[:half] + up.astype(F32), ahead[half:]], axis=0).astype(BF16)
    behind = pieces[3].astype(F32)
    behind = jnp.concatenate(
        [behind[:half], behind[half:] + down.astype(F32)], axis=0
    ).astype(BF16)
    ahead, behind, _ = lax.optimization_barrier((ahead, behind, ahead_of))
    from_behind = shift(ahead, axis, 1)
    from_ahead = shift(behind, axis, -1)
    return pieces[0].astype(F32) + from_behind.astype(F32) + from_ahead.astype(F32)


def pick(value, index):
    return lax.dynamic_index_in_dim(value, index, axis=0, keepdims=False)


def arrange(pieces, index):
    out = jnp.zeros((len(pieces),) + pieces[0].shape, pieces[0].dtype)
    for k, piece in enumerate(pieces):
        out = lax.dynamic_update_index_in_dim(out, piece, (index + k) % len(pieces), 0)
    return out


def body(
    tokens,
    router_weight,
    expert_ids,
    expert_gate,
    expert_up,
    expert_down,
    gate_weight,
    up_weight,
    down_weight,
):
    rows, width = tokens.shape
    experts_count = router_weight.shape[1]
    capacity = rows * expert_ids.shape[1] * 5 // (4 * experts_count)
    part, units = gate_weight.shape
    block = units // 4
    half = width // 2
    ix, iy, iz, ic = (lax.axis_index(a) for a in ("x", "y", "z", "core"))
    number = iz * 2 + ic

    def swap(value):
        return shift(value, "core", 1)

    chosen = expert_ids == number
    slot_index = local_slots(expert_ids, experts_count)
    slot_range = jnp.arange(capacity, dtype=jnp.int32)
    matches = chosen[None, :, :] & (slot_index[None, :, :] == slot_range[:, None, None])
    placing = jnp.any(matches, axis=2).astype(BF16)
    buffer = jnp.dot(placing, tokens, preferred_element_type=F32).astype(BF16)
    column = jnp.concatenate(gather_direct(buffer, "y"), axis=0)
    packed = jnp.stack(
        [
            jnp.concatenate(
                [
                    gate_weight[:, k * block : (k + 1) * block],
                    up_weight[:, k * block : (k + 1) * block],
                    down_weight[k * block : (k + 1) * block].T,
                ],
                axis=1,
            )
            for k in range(4)
        ]
    )
    weights_x = jnp.roll(lax.all_to_all(packed, "x", 0, 0), 2 * ic, axis=0)
    near_x = gather_near(column, "x")
    near_y = gather_near(weights_x, "y")
    far_x = after(gather_far(near_x, "x"), near_y)
    far_y = gather_far(near_y, "y")
    arrived = [column, near_x[1], far_x, near_x[0]]
    mixing = gate_mix(tokens, router_weight, expert_ids)
    weighting = jnp.sum(jnp.where(matches, mixing[None, :, :], 0.0), axis=2)
    weighting, _, _ = lax.optimization_barrier((weighting, arrived[1], arrived[3]))
    weighting = arrange(gather_direct(weighting, "x"), ix)
    weights = jnp.zeros((4, 4, part, 3 * block), BF16)
    for k, piece in enumerate([weights_x, near_y[1], far_y, near_y[0]]):
        weights = lax.dynamic_update_index_in_dim(weights, piece, (iy + k) % 4, 1)
    weights = weights.reshape(width, 3 * block)
    w_in = weights[:, : 2 * block]
    w_out = weights[:, 2 * block :]

    mine = lax.dynamic_slice_in_dim(tokens, ic * half, half, axis=1)
    quarter = lax.dynamic_slice_in_dim(mine, iz * (rows // 4), rows // 4, axis=0)
    quarter, _ = lax.optimization_barrier((quarter, column))
    quarter = arrange(gather_direct(quarter, "x"), ix)
    tokens_own = lax.all_gather(quarter.reshape(rows, half), "z", axis=0, tiled=True)
    tokens_all = jnp.concatenate([tokens_own, swap(tokens_own)], axis=1)
    w_gate, w_up, w_down = expert_gate[0], expert_up[0], expert_down[0]
    hidden_rows = []
    for rows_x in arrived:
        pre_gate = jnp.dot(rows_x, w_gate, preferred_element_type=F32)
        pre_up = jnp.dot(rows_x, w_up, preferred_element_type=F32)
        hidden_rows.append((jax.nn.silu(pre_gate) * pre_up).astype(BF16))
    hidden_x = arrange(hidden_rows, ix)
    hidden_x = after(hidden_x, weights)
    shares = [
        jnp.dot(
            hidden_x[:, k * capacity : (k + 1) * capacity].reshape(4 * capacity, -1),
            w_down,
            preferred_element_type=F32,
        ).astype(BF16)
        for k in range(4)
    ]

    pre = jnp.dot(tokens_all, w_in, preferred_element_type=F32)
    pre_act, up_proj = pre[:, :block], pre[:, block:]
    sig_gate = jax.nn.sigmoid(pre_act)
    active = pre_act * sig_gate
    hidden = (active * up_proj).astype(BF16)
    nt = (((1,), (1,)), ((), ()))
    tn = (((0,), (0,)), ((), ()))
    student = [
        lax.dot_general(hidden, w_out[rows_of], nt, preferred_element_type=F32)
        for rows_of in (slice(half, None), slice(0, half))
    ]

    expert_out = scatter_ring(shares, "y", student).reshape(4, capacity, width)

    def partial_value(base, core):
        teacher = lax.dot_general(
            weighting,
            lax.dynamic_slice_in_dim(expert_out, core * half, half, axis=2),
            (((1,), (1,)), ((0,), (0,))),
            precision=lax.Precision.HIGH,
            preferred_element_type=F32,
        )
        teacher = teacher.reshape(4, 4, rows // 4, half).transpose(1, 0, 2, 3)
        return base - teacher.reshape(base.shape)

    away = swap(partial_value(student[0], 1 - ic).astype(BF16))
    here = partial_value(student[1], ic) + away.astype(F32)
    here = lax.all_to_all(
        here.astype(BF16).reshape(16, rows // 4, half), ("z", "x"), 0, 0
    )
    total = jnp.sum(here.astype(F32), axis=0)
    token_total = rows * 16
    loss_scale = 1.0 / jnp.sqrt(jnp.float32(token_total))
    grad_out = (total * loss_scale).astype(BF16)
    grad_own = lax.all_to_all(
        jnp.broadcast_to(grad_out[None], (16,) + grad_out.shape), ("z", "x"), 0, 0
    ).reshape(4 * rows, half)
    grad_other = swap(grad_own)

    grad_down = jnp.concatenate(
        [
            lax.dot_general(g, hidden, tn, preferred_element_type=F32).astype(BF16)
            for g in (grad_own, grad_other)
        ],
        axis=0,
    )
    grad_other, grad_down = lax.optimization_barrier((grad_other, grad_down))
    grad_hidden = jnp.dot(grad_own, w_out[:half], preferred_element_type=F32) + jnp.dot(
        grad_other, w_out[half:], preferred_element_type=F32
    )
    grad_pre = (grad_hidden * up_proj * sig_gate * (1.0 + pre_act * (1.0 - sig_gate))).astype(
        BF16
    )
    grad_upper = (grad_hidden * active).astype(BF16)
    grad_gate = lax.dot_general(tokens_all, grad_pre, tn, preferred_element_type=F32).astype(BF16)
    grad_up = lax.dot_general(tokens_all, grad_upper, tn, preferred_element_type=F32).astype(BF16)

    def finish(grad):
        size = grad.shape[1]
        grad = grad.reshape(4, 4, part, size)
        pieces = [
            lax.dynamic_index_in_dim(grad, (iy + k) % 4, axis=1, keepdims=False)
            for k in range(4)
        ]
        summed = scatter_ring(pieces, "y")
        pieces = [
            lax.dynamic_index_in_dim(
                summed, ((ix + k) % 4) ^ (2 * ic), axis=0, keepdims=False
            ).astype(F32 if k == 0 else BF16)
            for k in range(4)
        ]
        parts = [p.astype(F32) for p in send_direct(pieces, "x")]
        return jnp.concatenate(
            [lax.select_n((place - ix) % 4, *parts) for place in range(4)], axis=1
        )

    down = finish(grad_down).T
    return (finish(grad_gate), finish(grad_up), down)


def solution(mesh):
    parts = Mesh(mesh.devices.reshape(4, 2, 4, 4), ("z", "core", "x", "y"))
    exp, fsdp = ("z", "core"), ("x", "y")
    return jax.shard_map(
        body,
        mesh=parts,
        in_specs=(
            P(fsdp, None),
            P(),
            P(fsdp, None),
            P(exp, None, fsdp),
            P(exp, None, fsdp),
            P(exp, fsdp, None),
            P(fsdp, exp),
            P(fsdp, exp),
            P(exp, fsdp),
        ),
        out_specs=(P(fsdp, exp), P(fsdp, exp), P(exp, fsdp)),
        check_vma=False,
    )
```

```python
import jax
import jax.numpy as jnp
from jax import lax
from jax.sharding import Mesh, PartitionSpec as P

F32 = jnp.float32
BF16 = jnp.bfloat16


def gate_mix(tokens, router_weight, expert_ids):
    logits = jnp.dot(tokens, router_weight, preferred_element_type=F32)
    experts_count = router_weight.shape[1]
    onehot = (
        expert_ids[:, :, None] == jnp.arange(experts_count, dtype=jnp.int32)[None, None, :]
    ).astype(F32)
    picked_logits = jnp.sum(onehot * logits[:, None, :], axis=2)
    return 1.0 / (1.0 + jnp.exp(picked_logits[:, ::-1] - picked_logits))


def local_slots(expert_ids, experts_count):
    pairs = expert_ids.shape[0] * expert_ids.shape[1]
    flat_ids = expert_ids.reshape(pairs)
    onehot = (flat_ids[:, None] == jnp.arange(experts_count, dtype=jnp.int32)[None, :]).astype(
        jnp.int32
    )
    before = jnp.cumsum(onehot, axis=0) - onehot
    return jnp.sum(before * onehot, axis=1).reshape(expert_ids.shape)


def shift(value, axis, step):
    size = lax.axis_size(axis)
    return lax.ppermute(value, axis, [(i, (i + step) % size) for i in range(size)])


def gather_direct(value, axis):
    return [value, shift(value, axis, -1), shift(value, axis, -2), shift(value, axis, -3)]


def after(value, *others):
    return lax.optimization_barrier((value, others))[0]


def gather_near(value, axis):
    return shift(value, axis, 1), shift(value, axis, -1)


def gather_far(near, axis):
    behind, ahead = near
    half = behind.shape[0] // 2
    return jnp.concatenate([shift(behind[:half], axis, 1), shift(ahead[half:], axis, -1)], axis=0)


def send_direct(pieces, axis):
    return [
        pieces[0],
        shift(pieces[3], axis, -1),
        shift(pieces[2], axis, -2),
        shift(pieces[1], axis, 1),
    ]


def scatter_direct(pieces, axis):
    own = pieces[0].astype(F32)
    sent = send_direct([None] + [p.astype(BF16) for p in pieces[1:]], axis)
    return own + sent[1].astype(F32) + sent[2].astype(F32) + sent[3].astype(F32)


def scatter_ring(pieces, axis, ahead_of=()):
    half = pieces[2].shape[0] // 2
    far = pieces[2].astype(BF16)
    up = shift(far[:half], axis, 1)
    down = shift(far[half:], axis, -1)
    ahead = pieces[1].astype(F32)
    ahead = jnp.concatenate([ahead[:half] + up.astype(F32), ahead[half:]], axis=0).astype(BF16)
    behind = pieces[3].astype(F32)
    behind = jnp.concatenate(
        [behind[:half], behind[half:] + down.astype(F32)], axis=0
    ).astype(BF16)
    ahead, behind, _ = lax.optimization_barrier((ahead, behind, ahead_of))
    from_behind = shift(ahead, axis, 1)
    from_ahead = shift(behind, axis, -1)
    return pieces[0].astype(F32) + from_behind.astype(F32) + from_ahead.astype(F32)


def pick(value, index):
    return lax.dynamic_index_in_dim(value, index, axis=0, keepdims=False)


def arrange(pieces, index):
    out = jnp.zeros((len(pieces),) + pieces[0].shape, pieces[0].dtype)
    for k, piece in enumerate(pieces):
        out = lax.dynamic_update_index_in_dim(out, piece, (index + k) % len(pieces), 0)
    return out


def body(
    tokens,
    router_weight,
    expert_ids,
    expert_gate,
    expert_up,
    expert_down,
    gate_weight,
    up_weight,
    down_weight,
):
    rows, width = tokens.shape
    experts_count = router_weight.shape[1]
    capacity = rows * expert_ids.shape[1] * 5 // (4 * experts_count)
    part, units = gate_weight.shape
    block = units // 4
    half = width // 2
    ix, iy, iz, ic = (lax.axis_index(a) for a in ("x", "y", "z", "core"))
    number = iz * 2 + ic

    def swap(value):
        return shift(value, "core", 1)

    chosen = expert_ids == number
    slot_index = local_slots(expert_ids, experts_count)
    slot_range = jnp.arange(capacity, dtype=jnp.int32)
    matches = chosen[None, :, :] & (slot_index[None, :, :] == slot_range[:, None, None])
    placing = jnp.any(matches, axis=2).astype(BF16)
    buffer = jnp.dot(placing, tokens, preferred_element_type=F32).astype(BF16)
    column = jnp.concatenate(gather_direct(buffer, "y"), axis=0)
    packed = jnp.stack(
        [
            jnp.concatenate(
                [
                    gate_weight[:, k * block : (k + 1) * block],
                    up_weight[:, k * block : (k + 1) * block],
                    down_weight[k * block : (k + 1) * block].T,
                ],
                axis=1,
            )
            for k in range(4)
        ]
    )
    weights_x = jnp.roll(lax.all_to_all(packed, "x", 0, 0), 2 * ic, axis=0)
    near_x = gather_near(column, "x")
    near_y = gather_near(weights_x, "y")
    far_x = after(gather_far(near_x, "x"), near_y)
    far_y = gather_far(near_y, "y")
    arrived = [column, near_x[1], far_x, near_x[0]]
    mixing = gate_mix(tokens, router_weight, expert_ids)
    weighting = jnp.sum(jnp.where(matches, mixing[None, :, :], 0.0), axis=2)
    weighting, _, _ = lax.optimization_barrier((weighting, arrived[1], arrived[3]))
    weighting = arrange(gather_direct(weighting, "x"), ix)
    weights = jnp.zeros((4, 4, part, 3 * block), BF16)
    for k, piece in enumerate([weights_x, near_y[1], far_y, near_y[0]]):
        weights = lax.dynamic_update_index_in_dim(weights, piece, (iy + k) % 4, 1)
    weights = weights.reshape(width, 3 * block)
    w_in = weights[:, : 2 * block]
    w_out = weights[:, 2 * block :]

    mine = lax.dynamic_slice_in_dim(tokens, ic * half, half, axis=1)
    quarter = lax.dynamic_slice_in_dim(mine, iz * (rows // 4), rows // 4, axis=0)
    quarter, _ = lax.optimization_barrier((quarter, column))
    quarter = arrange(gather_direct(quarter, "x"), ix)
    quarter = quarter.reshape(1, rows, half)
    tokens_own = lax.all_to_all(
        jnp.broadcast_to(quarter, (4, rows, half)), "z", 0, 0
    ).reshape(4 * rows, half)
    tokens_all = jnp.concatenate([tokens_own, swap(tokens_own)], axis=1)
    w_gate, w_up, w_down = expert_gate[0], expert_up[0], expert_down[0]
    hidden_rows = []
    for rows_x in arrived:
        pre_gate = jnp.dot(rows_x, w_gate, preferred_element_type=F32)
        pre_up = jnp.dot(rows_x, w_up, preferred_element_type=F32)
        hidden_rows.append((jax.nn.silu(pre_gate) * pre_up).astype(BF16))
    hidden_x = arrange(hidden_rows, ix)
    hidden_x = after(hidden_x, weights)
    shares = [
        jnp.dot(
            hidden_x[:, k * capacity : (k + 1) * capacity].reshape(4 * capacity, -1),
            w_down,
            preferred_element_type=F32,
        ).astype(BF16)
        for k in range(4)
    ]

    pre = jnp.dot(tokens_all, w_in, preferred_element_type=F32)
    pre_act, up_proj = pre[:, :block], pre[:, block:]
    sig_gate = jax.nn.sigmoid(pre_act)
    active = pre_act * sig_gate
    hidden = (active * up_proj).astype(BF16)
    nt = (((1,), (1,)), ((), ()))
    tn = (((0,), (0,)), ((), ()))
    student = [
        lax.dot_general(hidden, w_out[rows_of], nt, preferred_element_type=F32)
        for rows_of in (slice(half, None), slice(0, half))
    ]

    expert_out = scatter_ring(shares, "y", student).reshape(4, capacity, width)

    def partial_value(base, core):
        teacher = lax.dot_general(
            weighting,
            lax.dynamic_slice_in_dim(expert_out, core * half, half, axis=2),
            (((1,), (1,)), ((0,), (0,))),
            precision=lax.Precision.HIGH,
            preferred_element_type=F32,
        )
        teacher = teacher.reshape(4, 4, rows // 4, half).transpose(1, 0, 2, 3)
        return base - teacher.reshape(base.shape)

    away = swap(partial_value(student[0], 1 - ic).astype(BF16))
    here = partial_value(student[1], ic) + away.astype(F32)
    here = lax.all_to_all(
        here.astype(BF16).reshape(16, rows // 4, half), ("z", "x"), 0, 0
    )
    total = jnp.sum(here.astype(F32), axis=0)
    token_total = rows * 16
    loss_scale = 1.0 / jnp.sqrt(jnp.float32(token_total))
    grad_out = (total * loss_scale).astype(BF16)
    grad_own = lax.all_to_all(
        jnp.broadcast_to(grad_out[None], (16,) + grad_out.shape), ("z", "x"), 0, 0
    ).reshape(4 * rows, half)
    grad_other = swap(grad_own)

    grad_down = jnp.concatenate(
        [
            lax.dot_general(g, hidden, tn, preferred_element_type=F32).astype(BF16)
            for g in (grad_own, grad_other)
        ],
        axis=0,
    )
    grad_other, grad_down = lax.optimization_barrier((grad_other, grad_down))
    grad_hidden = jnp.dot(grad_own, w_out[:half], preferred_element_type=F32) + jnp.dot(
        grad_other, w_out[half:], preferred_element_type=F32
    )
    grad_pre = (grad_hidden * up_proj * sig_gate * (1.0 + pre_act * (1.0 - sig_gate))).astype(
        BF16
    )
    grad_upper = (grad_hidden * active).astype(BF16)
    grad_gate = lax.dot_general(tokens_all, grad_pre, tn, preferred_element_type=F32).astype(BF16)
    grad_up = lax.dot_general(tokens_all, grad_upper, tn, preferred_element_type=F32).astype(BF16)

    def finish(grad):
        size = grad.shape[1]
        grad = grad.reshape(4, 4, part, size)
        pieces = [
            lax.dynamic_index_in_dim(grad, (iy + k) % 4, axis=1, keepdims=False)
            for k in range(4)
        ]
        summed = scatter_ring(pieces, "y")
        pieces = [
            lax.dynamic_index_in_dim(
                summed, ((ix + k) % 4) ^ (2 * ic), axis=0, keepdims=False
            ).astype(F32 if k == 0 else BF16)
            for k in range(4)
        ]
        parts = [p.astype(F32) for p in send_direct(pieces, "x")]
        return jnp.concatenate(
            [lax.select_n((place - ix) % 4, *parts) for place in range(4)], axis=1
        )

    down = finish(grad_down).T
    return (finish(grad_gate), finish(grad_up), down)


def solution(mesh):
    parts = Mesh(mesh.devices.reshape(4, 2, 4, 4), ("z", "core", "x", "y"))
    exp, fsdp = ("z", "core"), ("x", "y")
    return jax.shard_map(
        body,
        mesh=parts,
        in_specs=(
            P(fsdp, None),
            P(),
            P(fsdp, None),
            P(exp, None, fsdp),
            P(exp, None, fsdp),
            P(exp, fsdp, None),
            P(fsdp, exp),
            P(fsdp, exp),
            P(exp, fsdp),
        ),
        out_specs=(P(fsdp, exp), P(fsdp, exp), P(exp, fsdp)),
        check_vma=False,
    )
```

```python
import jax
import jax.numpy as jnp
from jax import lax
from jax.sharding import Mesh, PartitionSpec as P

F32 = jnp.float32
BF16 = jnp.bfloat16


def gate_mix(tokens, router_weight, expert_ids):
    logits = jnp.dot(tokens, router_weight, preferred_element_type=F32)
    experts_count = router_weight.shape[1]
    onehot = (
        expert_ids[:, :, None] == jnp.arange(experts_count, dtype=jnp.int32)[None, None, :]
    ).astype(F32)
    picked_logits = jnp.sum(onehot * logits[:, None, :], axis=2)
    return 1.0 / (1.0 + jnp.exp(picked_logits[:, ::-1] - picked_logits))


def local_slots(expert_ids, experts_count):
    pairs = expert_ids.shape[0] * expert_ids.shape[1]
    flat_ids = expert_ids.reshape(pairs)
    onehot = (flat_ids[:, None] == jnp.arange(experts_count, dtype=jnp.int32)[None, :]).astype(
        jnp.int32
    )
    before = jnp.cumsum(onehot, axis=0) - onehot
    return jnp.sum(before * onehot, axis=1).reshape(expert_ids.shape)


def shift(value, axis, step):
    size = lax.axis_size(axis)
    return lax.ppermute(value, axis, [(i, (i + step) % size) for i in range(size)])


def gather_direct(value, axis):
    return [value, shift(value, axis, -1), shift(value, axis, -2), shift(value, axis, -3)]


def after(value, *others):
    return lax.optimization_barrier((value, others))[0]


def gather_near(value, axis):
    return shift(value, axis, 1), shift(value, axis, -1)


def gather_far(near, axis):
    behind, ahead = near
    half = behind.shape[0] // 2
    return jnp.concatenate([shift(behind[:half], axis, 1), shift(ahead[half:], axis, -1)], axis=0)


def send_direct(pieces, axis):
    return [
        pieces[0],
        shift(pieces[3], axis, -1),
        shift(pieces[2], axis, -2),
        shift(pieces[1], axis, 1),
    ]


def scatter_direct(pieces, axis):
    own = pieces[0].astype(F32)
    sent = send_direct([None] + [p.astype(BF16) for p in pieces[1:]], axis)
    return own + sent[1].astype(F32) + sent[2].astype(F32) + sent[3].astype(F32)


def scatter_ring(pieces, axis, ahead_of=()):
    half = pieces[2].shape[0] // 2
    far = pieces[2].astype(BF16)
    up = shift(far[:half], axis, 1)
    down = shift(far[half:], axis, -1)
    ahead = pieces[1].astype(F32)
    ahead = jnp.concatenate([ahead[:half] + up.astype(F32), ahead[half:]], axis=0).astype(BF16)
    behind = pieces[3].astype(F32)
    behind = jnp.concatenate(
        [behind[:half], behind[half:] + down.astype(F32)], axis=0
    ).astype(BF16)
    ahead, behind, _ = lax.optimization_barrier((ahead, behind, ahead_of))
    from_behind = shift(ahead, axis, 1)
    from_ahead = shift(behind, axis, -1)
    return pieces[0].astype(F32) + from_behind.astype(F32) + from_ahead.astype(F32)


def pick(value, index):
    return lax.dynamic_index_in_dim(value, index, axis=0, keepdims=False)


def arrange(pieces, index):
    out = jnp.zeros((len(pieces),) + pieces[0].shape, pieces[0].dtype)
    for k, piece in enumerate(pieces):
        out = lax.dynamic_update_index_in_dim(out, piece, (index + k) % len(pieces), 0)
    return out


def body(
    tokens,
    router_weight,
    expert_ids,
    expert_gate,
    expert_up,
    expert_down,
    gate_weight,
    up_weight,
    down_weight,
):
    rows, width = tokens.shape
    experts_count = router_weight.shape[1]
    capacity = rows * expert_ids.shape[1] * 5 // (4 * experts_count)
    part, units = gate_weight.shape
    block = units // 4
    half = width // 2
    ix, iy, iz, ic = (lax.axis_index(a) for a in ("x", "y", "z", "core"))
    number = iz * 2 + ic

    def swap(value):
        return shift(value, "core", 1)

    chosen = expert_ids == number
    slot_index = local_slots(expert_ids, experts_count)
    slot_range = jnp.arange(capacity, dtype=jnp.int32)
    matches = chosen[None, :, :] & (slot_index[None, :, :] == slot_range[:, None, None])
    placing = jnp.any(matches, axis=2).astype(BF16)
    buffer = jnp.dot(placing, tokens, preferred_element_type=F32).astype(BF16)
    column = jnp.concatenate(gather_direct(buffer, "y"), axis=0)
    packed = jnp.stack(
        [
            jnp.concatenate(
                [
                    gate_weight[:, k * block : (k + 1) * block],
                    up_weight[:, k * block : (k + 1) * block],
                    down_weight[k * block : (k + 1) * block].T,
                ],
                axis=1,
            )
            for k in range(4)
        ]
    )
    weights_x = lax.all_to_all(packed, "x", 0, 0)
    near_x = gather_near(column, "x")
    near_y = gather_near(weights_x, "y")
    far_x = after(gather_far(near_x, "x"), near_y)
    far_y = gather_far(near_y, "y")
    arrived = [column, near_x[1], far_x, near_x[0]]
    mixing = gate_mix(tokens, router_weight, expert_ids)
    weighting = jnp.sum(jnp.where(matches, mixing[None, :, :], 0.0), axis=2)
    weighting, _, _ = lax.optimization_barrier((weighting, arrived[1], arrived[3]))
    weighting = arrange(gather_direct(weighting, "x"), ix)
    weights = jnp.zeros((4, 4, part, 3 * block), BF16)
    for k, piece in enumerate([weights_x, near_y[1], far_y, near_y[0]]):
        weights = lax.dynamic_update_index_in_dim(weights, piece, (iy + k) % 4, 1)
    weights = weights.reshape(width, 3 * block)
    w_in = weights[:, : 2 * block]
    w_out = weights[:, 2 * block :]

    mine = lax.dynamic_slice_in_dim(tokens, ic * half, half, axis=1)
    quarter = lax.dynamic_slice_in_dim(mine, iz * (rows // 4), rows // 4, axis=0)
    quarter, _ = lax.optimization_barrier((quarter, column))
    quarter = arrange(gather_direct(quarter, "x"), ix)
    quarter = quarter.reshape(1, rows, half)
    tokens_own = lax.all_to_all(
        jnp.broadcast_to(quarter, (4, rows, half)), "z", 0, 0
    ).reshape(4 * rows, half)
    tokens_other = swap(tokens_own)

    def in_order(own, other, axis):
        return jnp.concatenate(
            [jnp.where(ic == 0, own, other), jnp.where(ic == 0, other, own)], axis=axis
        )

    def rows_of(value, core):
        return lax.dynamic_slice_in_dim(value, core * half, half, axis=0)

    tokens_all = in_order(tokens_own, tokens_other, 1)
    w_gate, w_up, w_down = expert_gate[0], expert_up[0], expert_down[0]
    hidden_rows = []
    for rows_x in arrived:
        pre_gate = jnp.dot(rows_x, w_gate, preferred_element_type=F32)
        pre_up = jnp.dot(rows_x, w_up, preferred_element_type=F32)
        hidden_rows.append((jax.nn.silu(pre_gate) * pre_up).astype(BF16))
    hidden_x = arrange(hidden_rows, ix)
    hidden_x = after(hidden_x, weights)
    shares = [
        jnp.dot(
            hidden_x[:, k * capacity : (k + 1) * capacity].reshape(4 * capacity, -1),
            w_down,
            preferred_element_type=F32,
        ).astype(BF16)
        for k in range(4)
    ]

    pre = jnp.dot(tokens_all, w_in, preferred_element_type=F32)
    pre_act, up_proj = pre[:, :block], pre[:, block:]
    sig_gate = jax.nn.sigmoid(pre_act)
    active = pre_act * sig_gate
    hidden = (active * up_proj).astype(BF16)
    nt = (((1,), (1,)), ((), ()))
    tn = (((0,), (0,)), ((), ()))
    student = [
        lax.dot_general(hidden, rows_of(w_out, core), nt, preferred_element_type=F32)
        for core in (1 - ic, ic)
    ]

    expert_out = scatter_ring(shares, "y", student).reshape(4, capacity, width)

    def partial_value(base, core):
        teacher = lax.dot_general(
            weighting,
            lax.dynamic_slice_in_dim(expert_out, core * half, half, axis=2),
            (((1,), (1,)), ((0,), (0,))),
            precision=lax.Precision.HIGH,
            preferred_element_type=F32,
        )
        teacher = teacher.reshape(4, 4, rows // 4, half).transpose(1, 0, 2, 3)
        return base - teacher.reshape(base.shape)

    away = swap(partial_value(student[0], 1 - ic).astype(BF16))
    here = partial_value(student[1], ic) + away.astype(F32)
    here = lax.all_to_all(
        here.astype(BF16).reshape(16, rows // 4, half), ("z", "x"), 0, 0
    )
    total = jnp.sum(here.astype(F32), axis=0)
    token_total = rows * 16
    loss_scale = 1.0 / jnp.sqrt(jnp.float32(token_total))
    grad_out = (total * loss_scale).astype(BF16)
    grad_own = lax.all_to_all(
        jnp.broadcast_to(grad_out[None], (16,) + grad_out.shape), ("z", "x"), 0, 0
    ).reshape(4 * rows, half)
    grad_other = swap(grad_own)

    grad_down = in_order(
        *[
            lax.dot_general(g, hidden, tn, preferred_element_type=F32).astype(BF16)
            for g in (grad_own, grad_other)
        ],
        0,
    )
    grad_other, grad_down = lax.optimization_barrier((grad_other, grad_down))
    grad_hidden = jnp.dot(
        grad_own, rows_of(w_out, ic), preferred_element_type=F32
    ) + jnp.dot(grad_other, rows_of(w_out, 1 - ic), preferred_element_type=F32)
    grad_pre = (grad_hidden * up_proj * sig_gate * (1.0 + pre_act * (1.0 - sig_gate))).astype(
        BF16
    )
    grad_upper = (grad_hidden * active).astype(BF16)
    grad_gate = lax.dot_general(tokens_all, grad_pre, tn, preferred_element_type=F32).astype(BF16)
    grad_up = lax.dot_general(tokens_all, grad_upper, tn, preferred_element_type=F32).astype(BF16)

    def finish(grad):
        size = grad.shape[1]
        grad = grad.reshape(4, 4, part, size)
        pieces = [
            lax.dynamic_index_in_dim(grad, (iy + k) % 4, axis=1, keepdims=False)
            for k in range(4)
        ]
        summed = scatter_ring(pieces, "y")
        pieces = [
            lax.dynamic_index_in_dim(
                summed, (ix + k) % 4, axis=0, keepdims=False
            ).astype(F32 if k == 0 else BF16)
            for k in range(4)
        ]
        parts = [p.astype(F32) for p in send_direct(pieces, "x")]
        return jnp.concatenate(
            [lax.select_n((place - ix) % 4, *parts) for place in range(4)], axis=1
        )

    down = finish(grad_down).T
    return (finish(grad_gate), finish(grad_up), down)


def solution(mesh):
    parts = Mesh(mesh.devices.reshape(4, 2, 4, 4), ("z", "core", "x", "y"))
    exp, fsdp = ("z", "core"), ("x", "y")
    return jax.shard_map(
        body,
        mesh=parts,
        in_specs=(
            P(fsdp, None),
            P(),
            P(fsdp, None),
            P(exp, None, fsdp),
            P(exp, None, fsdp),
            P(exp, fsdp, None),
            P(fsdp, exp),
            P(fsdp, exp),
            P(exp, fsdp),
        ),
        out_specs=(P(fsdp, exp), P(fsdp, exp), P(exp, fsdp)),
        check_vma=False,
    )
```
